32 devices in a mesh: chan: 8 (over z, y), grp: 4 (over x, core).
Axes of the slice: x: 2, y: 2, z: 4, core: 2. Of those that a mesh axis runs over, the one named last changes fastest.
Arguments:
- gate_up: bfloat16 [4096, 2, 28672], P('grp', None, 'chan'), may hold values from -6 to 6
- counts: int32 [4], P('grp'), may hold values from 512 to 1024
- panels: int32 [2, 512], replicated, may hold values from 0 to 28671, as said below
- inverses: float32 [2, 512, 512], replicated
- down_weight: bfloat16 [28672, 8192], P('chan', 'grp'), may hold values from -6 to 6
Outputs:
- pruned_weight: bfloat16 [28672, 8192], P('chan', 'grp')
The draws below stay inside these ranges and needn't reach their ends.
Inputs may be any that keep to these rules, and one draw needn't show every extreme that they name: `panels`: the entries 512 // 8 * s to 512 // 8 * (s + 1) - 1 of each panel lie in channels s * (28672 // 8) to (s + 1) * (28672 // 8) - 1; all 1024 indices are different.
All inputs are finite; a program needn't handle non-finite values.
Results may differ from the reference program's by a relative error of at most 0.0051.
Values may be sent and summed in bfloat16 or wider, within the bound.
A program may use at most 128 MiB of HBM per device.

```python
import math
import jax
import jax.numpy as jnp
from jax import lax

D = 8192
FF = 28672
PANEL = 512
TOK_DEV = 1024
TOKENS = 4096
N_CHAN = 8
N_GRP = 4


def draw_panels(key, part):
    local = FF // N_CHAN
    share = PANEL // N_CHAN
    keys = jax.random.split(key, N_CHAN)

    def choose(single):
        return jax.random.permutation(single, local)[:2 * share].astype(jnp.int32)
    picks = jax.vmap(choose)(keys)
    picks = picks + (jnp.arange(N_CHAN, dtype=jnp.int32) * local)[:, None]
    first_panel = picks[:, :share].reshape(-1)
    second_panel = picks[:, share:].reshape(-1)
    return jnp.stack([first_panel, second_panel]).astype(jnp.int32)


def draw_inverses(key, part):
    key_diag = jax.random.fold_in(key, 11)
    key_off = jax.random.fold_in(key, 12)
    diagonal = jax.random.uniform(key_diag, (2, PANEL), jnp.float32, 2.0, 6.0)
    off = jax.random.normal(key_off, (2, PANEL, PANEL), jnp.float32) * (1.5 / math.sqrt(PANEL))
    off = (off + jnp.swapaxes(off, 1, 2)) / math.sqrt(2.0)
    return (off + diagonal[:, :, None] * jnp.eye(PANEL, dtype=jnp.float32)[None]).astype(jnp.float32)


def plant(drawn, key, low, largest):
    longest = drawn.shape.index(max(drawn.shape))
    spots = []
    for shift in (0, 1):
        where = [jax.random.randint(jax.random.fold_in(key, axis), (), 0, length) for axis, length in enumerate(drawn.shape)]
        where[longest] = (where[longest] + shift) % drawn.shape[longest]
        spots.append(tuple(where))
    return drawn.at[spots[0]].set(low).at[spots[1]].set(largest)


def block_scale(rng, extent, shards, least, high):
    def one(position, blocks):
        heights = jax.random.uniform(jax.random.fold_in(jax.random.fold_in(rng, 6), position), (blocks,), jnp.float32, least / len(shards), high / len(shards))
        return jnp.repeat(jnp.exp(heights), extent[position] // blocks).reshape((-1,) + (1,) * (len(extent) - position - 1))

    gain = one(*shards[0])
    for cut in shards[1:]:
        gain = gain * one(*cut)
    return gain


def normal_values(key, extent, width, reach, cuts=(), kind=jnp.bfloat16):
    result = width * jax.random.normal(key, extent, jnp.float32)
    if cuts:
        result = result * block_scale(key, extent, cuts, -0.22, 0.18)
    return jnp.clip(result, -reach, reach).astype(kind)


def setup_inputs(seed: int = 0) -> dict:
    splits = jax.random.split(jax.random.key(seed), 6)
    return {
        "gate_up": normal_values(splits[0], (TOKENS, 2, FF), 1.0, 6.0, ((0, 4), (2, 8))),
        "counts": plant(jax.random.randint(splits[1], (N_GRP,), TOK_DEV // 2, TOK_DEV + 1), jax.random.fold_in(splits[1], 1), TOK_DEV // 2, TOK_DEV).astype(jnp.int32),
        "panels": draw_panels(jax.random.fold_in(splits[5], 71), 0),
        "inverses": draw_inverses(jax.random.fold_in(splits[5], 71), 0),
        "down_weight": normal_values(splits[4], (FF, D), 1.0, 6.0, ((0, 8), (1, 4))),
    }


def reference(gate_up, counts, panels, inverses, down_weight):
    slot = jnp.arange(TOKENS, dtype=jnp.int32)
    valid = (slot % TOK_DEV < jnp.repeat(counts, TOK_DEV)).astype(jnp.float32)
    total = jnp.sum(counts.astype(jnp.float32))
    gate_half = gate_up[:, 0, :].astype(jnp.float32)
    up_half = gate_up[:, 1, :].astype(jnp.float32)
    hidden = (jax.nn.silu(gate_half) * up_half * valid[:, None]).astype(jnp.bfloat16)
    weight = down_weight.astype(jnp.float32)
    for panel_no in range(2):
        picked = panels[panel_no]
        columns = jnp.take(hidden, picked, axis=1)
        hess = lax.dot_general(hidden, columns, (((0,), (0,)), ((), ())), preferred_element_type=jnp.float32) / total
        update = jnp.dot(inverses[panel_no], jnp.take(weight, picked, axis=0), precision=lax.Precision.HIGHEST)
        weight = weight - jnp.dot(hess, update, precision=lax.Precision.HIGHEST)
        removed = panels[:panel_no + 1].reshape(-1).astype(jnp.int32)
        weight = weight.at[removed].set(0.0)
    return weight.astype(jnp.bfloat16)
```

```python
import functools

import jax
import jax.numpy as jnp
from jax import lax
from jax.experimental import pallas as pl
from jax.experimental.pallas import tpu as pltpu
from jax.sharding import PartitionSpec as P

MESH = pl.DeviceIdType.MESH
NT = (((1,), (1,)), ((), ()))


def hidden_kernel(count_ref, x_ref, pick_ref, hidden_ref, acts_ref):
    rows = x_ref.shape[0]
    pairs = x_ref[...].reshape(2 * rows, x_ref.shape[2])
    row = lax.broadcasted_iota(jnp.int32, (rows, 2 * rows), 0)
    col = lax.broadcasted_iota(jnp.int32, (rows, 2 * rows), 1)
    gate = jnp.dot((col == 2 * row).astype(jnp.bfloat16), pairs, preferred_element_type=jnp.float32)
    up = jnp.dot((col == 2 * row + 1).astype(jnp.bfloat16), pairs, preferred_element_type=jnp.float32)
    slot = lax.broadcasted_iota(jnp.int32, (rows, 1), 0) + pl.program_id(0) * rows
    valid = (slot < count_ref[0]).astype(jnp.float32)
    hidden = (gate / (1.0 + jnp.exp(-gate)) * up * valid).astype(jnp.bfloat16)
    hidden_ref[...] = hidden
    acts_ref[...] = lax.dot_general(
        pick_ref[...], hidden, NT, preferred_element_type=jnp.float32
    ).astype(jnp.bfloat16)


def make_hidden(counts, gate_up, pick):
    tokens, _, local = gate_up.shape
    rows = 128
    return pl.pallas_call(
        hidden_kernel,
        grid_spec=pltpu.PrefetchScalarGridSpec(
            num_scalar_prefetch=1,
            grid=(tokens // rows,),
            in_specs=[
                pl.BlockSpec((rows, 2, local), lambda i, c: (i, 0, 0)),
                pl.BlockSpec(pick.shape, lambda i, c: (0, 0)),
            ],
            out_specs=[
                pl.BlockSpec((rows, local), lambda i, c: (i, 0)),
                pl.BlockSpec((pick.shape[0], rows), lambda i, c: (0, i)),
            ],
        ),
        out_shape=[
            jax.ShapeDtypeStruct((tokens, local), jnp.bfloat16),
            jax.ShapeDtypeStruct((pick.shape[0], tokens), jnp.bfloat16),
        ],
        compiler_params=pltpu.CompilerParams(vmem_limit_bytes=48 << 20),
    )(counts, gate_up, pick)


def hessian_kernel(
    n, chunk, hidden_ref, own_ref, count_ref, hess_ref, cross_ref, total_ref,
    acts, part, core_out, core_in, line_out, line_in, done, cpart, cin, call,
    push_sem, fwd_sem, acts_sem, core_ssem, core_rsem, line_ssem, line_rsem,
    done_ssem, done_rsem, local_sem, cpart_ssem, cpart_rsem, call_ssem, call_rsem,
):
    chan, grp = lax.axis_index("chan"), lax.axis_index("grp")
    half = n // 2
    z, y = chan // 2, chan % 2
    line, core = grp // 2, grp % 2
    share, local = line_out.shape[1], line_out.shape[2]
    beside = {"chan": z * 2 + (1 - y)}
    other_core = {"grp": line * 2 + (1 - core)}
    other_line = {"grp": (1 - line) * 2 + core}

    barrier = pltpu.get_barrier_semaphore()

    def greet(j, _):
        pl.semaphore_signal(barrier, inc=1, device_id={"chan": (chan + j) % n}, device_id_type=MESH)
        return 0

    lax.fori_loop(1, n, greet, 0)
    for j in range(1, 4):
        pl.semaphore_signal(barrier, inc=1, device_id={"grp": (grp + j) % 4}, device_id_type=MESH)
    pl.semaphore_wait(barrier, n - 1 + 3)

    def remote(src, dst, ssem, rsem, where):
        return pltpu.make_async_remote_copy(
            src_ref=src, dst_ref=dst, send_sem=ssem, recv_sem=rsem,
            device_id=where, device_id_type=MESH)

    def block_at(k):
        return ((z + half - k // 2) % half) * 2 + (y + k) % 2

    def push(j):
        where = beside if j is None else {"chan": ((z + j) % half) * 2 + y}
        sem = push_sem.at[0 if j is None else j]
        return remote(own_ref, acts.at[chan], sem, acts_sem.at[chan], where)

    def forward(k):
        b = block_at(k)
        return remote(acts.at[b], acts.at[b], fwd_sem.at[k // 2], acts_sem.at[b], beside)

    def start_push(j, _):
        push(j).start()
        return 0

    def wait_push(j, _):
        push(j).wait_send()
        return 0

    push(None).start()
    lax.fori_loop(1, half, start_push, 0)
    keep = pltpu.make_async_copy(own_ref, acts.at[chan], local_sem.at[n])
    keep.start()
    keep.wait()

    def arrived(b):
        remote(own_ref, acts.at[b], push_sem.at[0], acts_sem.at[b], beside).wait_recv()

    def to_core(b):
        return remote(core_out.at[b], core_in.at[b], core_ssem.at[b], core_rsem.at[b], other_core)

    def to_line(b):
        return remote(line_out.at[b], line_in.at[b], line_ssem.at[b], line_rsem.at[b], other_line)

    def to_done(b):
        return remote(done.at[b], hess_ref.at[b, core], done_ssem.at[b], done_rsem.at[b], other_core)

    def from_done(b):
        return remote(done.at[b], hess_ref.at[b, 1 - core], done_ssem.at[b], done_rsem.at[b], other_core)

    def to_own(b):
        return pltpu.make_async_copy(done.at[b], hess_ref.at[b, core], local_sem.at[b])

    def product(k):
        b = block_at(k)
        left = acts[b].reshape(2 * share, acts.shape[3])

        def tile(t, _):
            at = pl.ds(pl.multiple_of(t * chunk, chunk), chunk)
            both = jnp.dot(left, hidden_ref[:, at], preferred_element_type=jnp.float32)
            low, high = both[:share], both[share:]
            part[k % 2, :, at] = jnp.where(core == 0, low, high)
            core_out[b, :, at] = jnp.where(core == 0, high, low).astype(jnp.bfloat16)
            return 0

        lax.fori_loop(0, local // chunk, tile, 0)
        to_core(b).start()

    def pair(k):
        b = block_at(k)
        to_core(b).wait_recv()

        def tile(t, _):
            at = pl.ds(pl.multiple_of(t * chunk, chunk), chunk)
            line_out[b, :, at] = (part[k % 2, :, at] + core_in[b, :, at].astype(jnp.float32)).astype(jnp.bfloat16)
            return 0

        lax.fori_loop(0, local // chunk, tile, 0)
        to_line(b).start()

    def finish(k):
        b = block_at(k)
        to_line(b).wait_recv()

        def tile(t, _):
            at = pl.ds(pl.multiple_of(t * chunk, chunk), chunk)
            done[b, :, at] = (
                line_out[b, :, at].astype(jnp.float32) + line_in[b, :, at].astype(jnp.float32)
            ).astype(jnp.bfloat16)
            return 0

        lax.fori_loop(0, local // chunk, tile, 0)
        to_done(b).start()
        to_own(b).start()

    def relay(h, _):
        arrived(block_at(2 * h))
        forward(2 * h).start()
        return 0

    product(0)
    arrived(block_at(1))
    product(1)
    pair(0)
    lax.fori_loop(1, half, relay, 0)
    pair(1)

    def gather(h, _):
        arrived(block_at(2 * h + 1))
        return 0

    def steps(k, _):
        product(k)
        pair(k - 1)
        finish(k - 2)
        return 0

    lax.fori_loop(1, half, gather, 0)

    first = acts[:, 0].reshape(n * share, acts.shape[3])
    cpart[:share] = lax.dot_general(acts[chan, 1], first, NT, preferred_element_type=jnp.float32)
    cpart[share:] = jnp.broadcast_to(count_ref[:, :1], (8, n * share))

    def to_group(j):
        return remote(cpart, cin.at[j - 1], cpart_ssem.at[j - 1], cpart_rsem.at[j - 1], {"grp": (grp + j) % 4})

    for j in range(1, 4):
        to_group(j).start()

    product(2)
    finish(0)
    lax.fori_loop(3, min(5, n), steps, 0)

    for j in range(1, 4):
        to_group(j).wait_recv()
    total = cpart[share:] + cin[0, share:] + cin[1, share:] + cin[2, share:]
    call[chan] = (cpart[:share] + cin[0, :share] + cin[1, :share] + cin[2, :share]) / total[:1]
    total_ref[...] = total[:, :128]

    def to_chan(j):
        return remote(call.at[chan], call.at[chan], call_ssem.at[j], call_rsem.at[chan], {"chan": (chan + j) % n})

    def start_chan(j, _):
        to_chan(j).start()
        return 0

    lax.fori_loop(1, n, start_chan, 0)
    lax.fori_loop(5, n, steps, 0)
    pair(n - 1)
    finish(n - 2)

    def end_chan(j, _):
        b = (chan + j) % n
        remote(call.at[chan], call.at[b], call_ssem.at[j], call_rsem.at[b], {"chan": b}).wait_recv()
        to_chan(j).wait_send()
        return 0

    lax.fori_loop(1, n, end_chan, 0)
    cross_ref[...] = call[...]
    finish(n - 1)

    push(None).wait_send()
    lax.fori_loop(1, half, wait_push, 0)
    for j in range(1, 4):
        to_group(j).wait_send()

    def end_forward(h, _):
        forward(2 * h).wait_send()
        return 0

    lax.fori_loop(1, half, end_forward, 0)

    def end_block(b, _):
        to_core(b).wait_send()
        to_line(b).wait_send()
        to_done(b).wait_send()
        from_done(b).wait_recv()
        to_own(b).wait()
        return 0

    lax.fori_loop(0, n, end_block, 0)


def make_hessian(n, hidden, own, count):
    tokens, local = hidden.shape
    share = own.shape[1]
    chunk = 512 if local % 512 == 0 else local
    vmem = pl.BlockSpec(memory_space=pltpu.VMEM)
    blocks = pltpu.VMEM((n, share, local), jnp.bfloat16)
    dma = pltpu.SemaphoreType.DMA
    return pl.pallas_call(
        functools.partial(hessian_kernel, n, chunk),
        in_specs=[vmem, vmem, vmem],
        out_specs=[pl.BlockSpec(memory_space=pl.ANY), vmem, vmem],
        out_shape=[
            jax.ShapeDtypeStruct((n, 2, share, local), jnp.bfloat16),
            jax.ShapeDtypeStruct((n, share, n * share), jnp.float32),
            jax.ShapeDtypeStruct((8, 128), jnp.float32),
        ],
        scratch_shapes=[
            pltpu.VMEM((n, 2, share, tokens), jnp.bfloat16),
            pltpu.VMEM((2, share, local), jnp.float32),
            blocks, blocks, blocks, blocks, blocks,
            pltpu.VMEM((share + 8, n * share), jnp.float32),
            pltpu.VMEM((3, share + 8, n * share), jnp.float32),
            pltpu.VMEM((n, share, n * share), jnp.float32),
            dma((n // 2,)), dma((n // 2,)), dma((n,)), dma((n,)), dma((n,)), dma((n,)), dma((n,)),
            dma((n,)), dma((n,)), dma((n + 1,)), dma((3,)), dma((3,)), dma((n,)), dma((n,)),
        ],
        compiler_params=pltpu.CompilerParams(
            collective_id=0, has_side_effects=True, vmem_limit_bytes=56 << 20
        ),
    )(hidden, own, count)


def body(gate_up, counts, panels, inverses, down_weight):
    tokens, _, local = gate_up.shape
    n = lax.axis_size("chan")
    share = panels.shape[1] // n
    columns = down_weight.shape[1]
    shard = lax.axis_index("chan")
    picked = lax.dynamic_slice(panels, (0, shard * share), (2, share)) - shard * local
    hits = picked.reshape(2 * share)[:, None] == jnp.arange(local, dtype=jnp.int32)[None, :]
    pick = hits.astype(jnp.bfloat16)
    kept = jnp.logical_not(jnp.any(hits, axis=0))
    rows = jnp.dot(pick, down_weight, preferred_element_type=jnp.float32).astype(jnp.bfloat16)
    rows = lax.all_gather(rows, "chan", axis=0, tiled=False).reshape(n, 2, share, columns)
    hidden, acts = make_hidden(counts, gate_up, pick)
    count = jnp.broadcast_to(counts.astype(jnp.float32)[:, None], (8, 128))
    hess, cross, total = make_hessian(n, hidden, acts.reshape(2, share, tokens), count)
    width = n * share
    high = lax.Precision.HIGH
    first_rows = rows[:, 0].reshape(width, columns).astype(jnp.float32)
    second_rows = rows[:, 1].reshape(width, columns).astype(jnp.float32)
    first = jnp.dot(inverses[0], first_rows, precision=high)
    second = second_rows - jnp.dot(cross.reshape(width, width), first, precision=high)
    second = jnp.dot(inverses[1], second, precision=high)
    update = jnp.stack((first.reshape(n, share, columns), second.reshape(n, share, columns)), axis=1)
    update = (update / total[0, 0]).astype(jnp.bfloat16).reshape(2 * width, columns)
    change = lax.dot_general(
        hess.reshape(2 * width, local), update, (((0,), (0,)), ((), ())), preferred_element_type=jnp.float32
    )
    weight = jnp.where(kept[:, None], down_weight.astype(jnp.float32) - change, 0.0)
    return weight.astype(jnp.bfloat16)


def solution(mesh):
    in_specs = (P("grp", None, "chan"), P("grp"), P(), P(), P("chan", "grp"))
    out_specs = P("chan", "grp")
    return jax.shard_map(body, mesh=mesh, in_specs=in_specs, out_specs=out_specs, check_vma=False)
```

```python
import functools

import jax
import jax.numpy as jnp
from jax import lax
from jax.experimental import pallas as pl
from jax.experimental.pallas import tpu as pltpu
from jax.sharding import PartitionSpec as P

MESH = pl.DeviceIdType.MESH
NT = (((1,), (1,)), ((), ()))


def hidden_kernel(count_ref, x_ref, pick_ref, hidden_ref, acts_ref):
    rows = x_ref.shape[0]
    pairs = x_ref[...].reshape(2 * rows, x_ref.shape[2])
    row = lax.broadcasted_iota(jnp.int32, (rows, 2 * rows), 0)
    col = lax.broadcasted_iota(jnp.int32, (rows, 2 * rows), 1)
    gate = jnp.dot((col == 2 * row).astype(jnp.bfloat16), pairs, preferred_element_type=jnp.float32)
    up = jnp.dot((col == 2 * row + 1).astype(jnp.bfloat16), pairs, preferred_element_type=jnp.float32)
    slot = lax.broadcasted_iota(jnp.int32, (rows, 1), 0) + pl.program_id(0) * rows
    valid = (slot < count_ref[0]).astype(jnp.float32)
    hidden = (gate / (1.0 + jnp.exp(-gate)) * up * valid).astype(jnp.bfloat16)
    hidden_ref[...] = hidden
    acts_ref[...] = lax.dot_general(
        pick_ref[...], hidden, NT, preferred_element_type=jnp.float32
    ).astype(jnp.bfloat16)


def make_hidden(counts, gate_up, pick):
    tokens, _, local = gate_up.shape
    rows = 128
    return pl.pallas_call(
        hidden_kernel,
        grid_spec=pltpu.PrefetchScalarGridSpec(
            num_scalar_prefetch=1,
            grid=(tokens // rows,),
            in_specs=[
                pl.BlockSpec((rows, 2, local), lambda i, c: (i, 0, 0)),
                pl.BlockSpec(pick.shape, lambda i, c: (0, 0)),
            ],
            out_specs=[
                pl.BlockSpec((rows, local), lambda i, c: (i, 0)),
                pl.BlockSpec((pick.shape[0], rows), lambda i, c: (0, i)),
            ],
        ),
        out_shape=[
            jax.ShapeDtypeStruct((tokens, local), jnp.bfloat16),
            jax.ShapeDtypeStruct((pick.shape[0], tokens), jnp.bfloat16),
        ],
        compiler_params=pltpu.CompilerParams(vmem_limit_bytes=48 << 20),
    )(counts, gate_up, pick)


def hessian_kernel(
    n, chunk, hidden_ref, own_ref, count_ref, rows_ref, hess_ref, cross_ref, total_ref, all_rows_ref,
    acts, part, core_out, core_in, line_out, line_in, done, cpart, cin, call,
    push_sem, fwd_sem, acts_sem, core_ssem, core_rsem, line_ssem, line_rsem,
    done_ssem, done_rsem, local_sem, cpart_ssem, cpart_rsem, call_ssem, call_rsem,
    row_push, row_fwd, row_sem, row_local,
):
    chan, grp = lax.axis_index("chan"), lax.axis_index("grp")
    half = n // 2
    z, y = chan // 2, chan % 2
    line, core = grp // 2, grp % 2
    share, local = line_out.shape[1], line_out.shape[2]
    beside = {"chan": z * 2 + (1 - y)}
    other_core = {"grp": line * 2 + (1 - core)}
    other_line = {"grp": (1 - line) * 2 + core}

    barrier = pltpu.get_barrier_semaphore()

    def greet(j, _):
        pl.semaphore_signal(barrier, inc=1, device_id={"chan": (chan + j) % n}, device_id_type=MESH)
        return 0

    lax.fori_loop(1, n, greet, 0)
    for j in range(1, 4):
        pl.semaphore_signal(barrier, inc=1, device_id={"grp": (grp + j) % 4}, device_id_type=MESH)
    pl.semaphore_wait(barrier, n - 1 + 3)

    def remote(src, dst, ssem, rsem, where):
        return pltpu.make_async_remote_copy(
            src_ref=src, dst_ref=dst, send_sem=ssem, recv_sem=rsem,
            device_id=where, device_id_type=MESH)

    def block_at(k):
        return ((z + half - k // 2) % half) * 2 + (y + k) % 2

    def push(j):
        where = beside if j is None else {"chan": ((z + j) % half) * 2 + y}
        sem = push_sem.at[0 if j is None else j]
        return remote(own_ref, acts.at[chan], sem, acts_sem.at[chan], where)

    def forward(k):
        b = block_at(k)
        return remote(acts.at[b], acts.at[b], fwd_sem.at[k // 2], acts_sem.at[b], beside)

    def start_push(j, _):
        push(j).start()
        return 0

    def wait_push(j, _):
        push(j).wait_send()
        return 0

    push(None).start()
    lax.fori_loop(1, half, start_push, 0)
    keep = pltpu.make_async_copy(own_ref, acts.at[chan], local_sem.at[n])
    keep.start()
    keep.wait()

    def arrived(b):
        remote(own_ref, acts.at[b], push_sem.at[0], acts_sem.at[b], beside).wait_recv()

    def to_core(b):
        return remote(core_out.at[b], core_in.at[b], core_ssem.at[b], core_rsem.at[b], other_core)

    def to_line(b):
        return remote(line_out.at[b], line_in.at[b], line_ssem.at[b], line_rsem.at[b], other_line)

    def to_done(b):
        return remote(done.at[b], hess_ref.at[b, core], done_ssem.at[b], done_rsem.at[b], other_core)

    def from_done(b):
        return remote(done.at[b], hess_ref.at[b, 1 - core], done_ssem.at[b], done_rsem.at[b], other_core)

    def to_own(b):
        return pltpu.make_async_copy(done.at[b], hess_ref.at[b, core], local_sem.at[b])

    def product(k):
        b = block_at(k)
        left = acts[b].reshape(2 * share, acts.shape[3])

        def tile(t, _):
            at = pl.ds(pl.multiple_of(t * chunk, chunk), chunk)
            both = jnp.dot(left, hidden_ref[:, at], preferred_element_type=jnp.float32)
            low, high = both[:share], both[share:]
            part[k % 2, :, at] = jnp.where(core == 0, low, high)
            core_out[b, :, at] = jnp.where(core == 0, high, low).astype(jnp.bfloat16)
            return 0

        lax.fori_loop(0, local // chunk, tile, 0)
        to_core(b).start()

    def pair(k):
        b = block_at(k)
        to_core(b).wait_recv()

        def tile(t, _):
            at = pl.ds(pl.multiple_of(t * chunk, chunk), chunk)
            line_out[b, :, at] = (part[k % 2, :, at] + core_in[b, :, at].astype(jnp.float32)).astype(jnp.bfloat16)
            return 0

        lax.fori_loop(0, local // chunk, tile, 0)
        to_line(b).start()

    def finish(k):
        b = block_at(k)
        to_line(b).wait_recv()

        def tile(t, _):
            at = pl.ds(pl.multiple_of(t * chunk, chunk), chunk)
            done[b, :, at] = (
                line_out[b, :, at].astype(jnp.float32) + line_in[b, :, at].astype(jnp.float32)
            ).astype(jnp.bfloat16)
            return 0

        lax.fori_loop(0, local // chunk, tile, 0)
        to_done(b).start()
        to_own(b).start()

    def relay(h, _):
        arrived(block_at(2 * h))
        forward(2 * h).start()
        return 0

    def gather(h, _):
        arrived(block_at(2 * h + 1))
        return 0

    def steps(k, _):
        product(k)
        pair(k - 1)
        finish(k - 2)
        return 0

    def rows_push(j):
        where = beside if j is None else {"chan": ((z + j) % half) * 2 + y}
        sem = row_push.at[0 if j is None else j]
        return remote(rows_ref, all_rows_ref.at[chan], sem, row_sem.at[chan], where)

    def rows_arrived(b):
        remote(rows_ref, all_rows_ref.at[b], row_push.at[0], row_sem.at[b], beside).wait_recv()

    def rows_forward(h):
        b = block_at(2 * h)
        return remote(all_rows_ref.at[b], all_rows_ref.at[b], row_fwd.at[h], row_sem.at[b], beside)

    def start_rows(j, _):
        rows_push(j).start()
        return 0

    def relay_rows(h, _):
        rows_arrived(block_at(2 * h))
        rows_forward(h).start()
        return 0

    def end_rows(h, _):
        rows_arrived(block_at(2 * h + 1))
        return 0

    def end_push(h, _):
        rows_push(h).wait_send()
        rows_forward(h).wait_send()
        return 0

    product(0)
    arrived(block_at(1))
    product(1)
    pair(0)
    lax.fori_loop(1, 2, relay, 0)
    product(2)
    pair(1)
    arrived(block_at(3))
    product(3)
    pair(2)
    lax.fori_loop(2, half, relay, 0)
    finish(0)
    lax.fori_loop(2, half, gather, 0)
    rows_push(None).start()
    lax.fori_loop(1, half, start_rows, 0)
    keep_rows = pltpu.make_async_copy(rows_ref, all_rows_ref.at[chan], row_local)
    keep_rows.start()

    first = acts[:, 0].reshape(n * share, acts.shape[3])
    cpart[:share] = lax.dot_general(acts[chan, 1], first, NT, preferred_element_type=jnp.float32)
    cpart[share:] = jnp.broadcast_to(count_ref[:, :1], (8, n * share))

    def to_group(j):
        return remote(cpart, cin.at[j - 1], cpart_ssem.at[j - 1], cpart_rsem.at[j - 1], {"grp": (grp + j) % 4})

    for j in range(1, 4):
        to_group(j).start()

    finish(1)
    lax.fori_loop(4, 5, steps, 0)

    for j in range(1, 4):
        to_group(j).wait_recv()
    total = cpart[share:] + cin[0, share:] + cin[1, share:] + cin[2, share:]
    call[chan] = (cpart[:share] + cin[0, :share] + cin[1, :share] + cin[2, :share]) / total[:1]
    total_ref[...] = total[:, :128]

    def to_chan(j):
        return remote(call.at[chan], call.at[chan], call_ssem.at[j], call_rsem.at[chan], {"chan": (chan + j) % n})

    def start_chan(j, _):
        to_chan(j).start()
        return 0

    lax.fori_loop(1, n, start_chan, 0)
    def late_steps(k, _):
        steps(k, 0)
        relay_rows(k - 4, 0)
        return 0

    middle = max(5, min(half + 4, n))
    lax.fori_loop(5, middle, late_steps, 0)
    lax.fori_loop(middle, n, steps, 0)
    lax.fori_loop(middle - 4, half, relay_rows, 0)
    pair(n - 1)
    finish(n - 2)

    def end_chan(j, _):
        b = (chan + j) % n
        remote(call.at[chan], call.at[b], call_ssem.at[j], call_rsem.at[b], {"chan": b}).wait_recv()
        to_chan(j).wait_send()
        return 0

    lax.fori_loop(1, n, end_chan, 0)
    cross_ref[...] = call[...]
    finish(n - 1)
    lax.fori_loop(0, half, end_rows, 0)
    rows_push(None).wait_send()
    lax.fori_loop(1, half, end_push, 0)
    keep_rows.wait()

    push(None).wait_send()
    lax.fori_loop(1, half, wait_push, 0)
    for j in range(1, 4):
        to_group(j).wait_send()

    def end_forward(h, _):
        forward(2 * h).wait_send()
        return 0

    lax.fori_loop(1, half, end_forward, 0)

    def end_block(b, _):
        to_core(b).wait_send()
        to_line(b).wait_send()
        to_done(b).wait_send()
        from_done(b).wait_recv()
        to_own(b).wait()
        return 0

    lax.fori_loop(0, n, end_block, 0)


def make_hessian(n, hidden, own, count, rows):
    tokens, local = hidden.shape
    share = own.shape[1]
    chunk = 512 if local % 512 == 0 else local
    vmem = pl.BlockSpec(memory_space=pltpu.VMEM)
    blocks = pltpu.VMEM((n, share, local), jnp.bfloat16)
    dma = pltpu.SemaphoreType.DMA
    return pl.pallas_call(
        functools.partial(hessian_kernel, n, chunk),
        in_specs=[vmem, vmem, vmem, vmem],
        out_specs=[pl.BlockSpec(memory_space=pl.ANY), vmem, vmem, pl.BlockSpec(memory_space=pl.ANY)],
        out_shape=[
            jax.ShapeDtypeStruct((n, 2, share, local), jnp.bfloat16),
            jax.ShapeDtypeStruct((n, share, n * share), jnp.float32),
            jax.ShapeDtypeStruct((8, 128), jnp.float32),
            jax.ShapeDtypeStruct((n,) + rows.shape, jnp.bfloat16),
        ],
        scratch_shapes=[
            pltpu.VMEM((n, 2, share, tokens), jnp.bfloat16),
            pltpu.VMEM((2, share, local), jnp.float32),
            blocks, blocks, blocks, blocks, blocks,
            pltpu.VMEM((share + 8, n * share), jnp.float32),
            pltpu.VMEM((3, share + 8, n * share), jnp.float32),
            pltpu.VMEM((n, share, n * share), jnp.float32),
            dma((n // 2,)), dma((n // 2,)), dma((n,)), dma((n,)), dma((n,)), dma((n,)), dma((n,)),
            dma((n,)), dma((n,)), dma((n + 1,)), dma((3,)), dma((3,)), dma((n,)), dma((n,)),
            dma((n // 2,)), dma((n // 2,)), dma((n,)), dma(()),
        ],
        compiler_params=pltpu.CompilerParams(
            collective_id=0, has_side_effects=True, vmem_limit_bytes=56 << 20
        ),
    )(hidden, own, count, rows)


def compensate_kernel(
    hess_ref, cross_ref, total_ref, rows_ref, inverses_ref, weight_ref, kept_ref, out_ref, update_ref
):
    n, _, share, columns = rows_ref.shape
    width = n * share
    step = min(512, columns)
    spans = [slice(t * step, (t + 1) * step) for t in range(columns // step)]

    def dot(a, b):
        return jnp.dot(a, b, preferred_element_type=jnp.float32)

    @pl.when(pl.program_id(0) == 0)
    def _():
        top = inverses_ref[0]
        coarse = top.astype(jnp.bfloat16)
        fine = (top - coarse.astype(jnp.float32)).astype(jnp.bfloat16)
        low = inverses_ref[1].astype(jnp.bfloat16)
        cross = cross_ref[...].reshape(width, width).astype(jnp.bfloat16)
        scale = 1.0 / total_ref[:1, :1]
        for at in spans:
            rows = rows_ref[:, 0, :, at].reshape(width, step)
            first = dot(coarse, rows) + dot(fine, rows)
            second = rows_ref[:, 1, :, at].reshape(width, step).astype(jnp.float32)
            second = dot(low, (second - dot(cross, first.astype(jnp.bfloat16))).astype(jnp.bfloat16))
            update_ref[:, 0, :, at] = (first * scale).reshape(n, share, step).astype(jnp.bfloat16)
            update_ref[:, 1, :, at] = (second * scale).reshape(n, share, step).astype(jnp.bfloat16)

    left = hess_ref[...].reshape(2 * width, hess_ref.shape[3]).T
    kept = kept_ref[...] > 0.5
    for at in spans:
        change = dot(left, update_ref[:, :, :, at].reshape(2 * width, step))
        out_ref[:, at] = jnp.where(kept, weight_ref[:, at].astype(jnp.float32) - change, 0.0).astype(jnp.bfloat16)


def compensate(hess, cross, total, rows, inverses, weight, kept):
    local, columns = weight.shape
    block = 256 if local % 256 == 0 else local

    def whole(array):
        return pl.BlockSpec(array.shape, lambda i: (0,) * array.ndim)

    return pl.pallas_call(
        compensate_kernel,
        grid=(local // block,),
        in_specs=[
            pl.BlockSpec(hess.shape[:3] + (block,), lambda i: (0, 0, 0, i)),
            whole(cross), whole(total), whole(rows), whole(inverses),
            pl.BlockSpec((block, columns), lambda i: (i, 0)),
            pl.BlockSpec((block, 1), lambda i: (i, 0)),
        ],
        out_specs=pl.BlockSpec((block, columns), lambda i: (i, 0)),
        out_shape=jax.ShapeDtypeStruct(weight.shape, jnp.bfloat16),
        scratch_shapes=[pltpu.VMEM(rows.shape, jnp.bfloat16)],
        compiler_params=pltpu.CompilerParams(vmem_limit_bytes=56 << 20),
    )(hess, cross, total, rows, inverses, weight, kept.astype(jnp.float32)[:, None])


def body(gate_up, counts, panels, inverses, down_weight):
    tokens, _, local = gate_up.shape
    n = lax.axis_size("chan")
    share = panels.shape[1] // n
    columns = down_weight.shape[1]
    shard = lax.axis_index("chan")
    picked = lax.dynamic_slice(panels, (0, shard * share), (2, share)) - shard * local
    hits = picked.reshape(2 * share)[:, None] == jnp.arange(local, dtype=jnp.int32)[None, :]
    pick = hits.astype(jnp.bfloat16)
    kept = jnp.logical_not(jnp.any(hits, axis=0))
    rows = jnp.dot(pick, down_weight, preferred_element_type=jnp.float32).astype(jnp.bfloat16)
    hidden, acts = make_hidden(counts, gate_up, pick)
    count = jnp.broadcast_to(counts.astype(jnp.float32)[:, None], (8, 128))
    hess, cross, total, rows = make_hessian(
        n, hidden, acts.reshape(2, share, tokens), count, rows.reshape(2, share, columns)
    )
    return compensate(hess, cross, total, rows, inverses, down_weight, kept)


def solution(mesh):
    in_specs = (P("grp", None, "chan"), P("grp"), P(), P(), P("chan", "grp"))
    out_specs = P("chan", "grp")
    return jax.shard_map(body, mesh=mesh, in_specs=in_specs, out_specs=out_specs, check_vma=False)
```
